256 devices in a mesh: spin: 2 (over core), dom: 128 (over x, z, y).
Axes of the slice: x: 4, y: 4, z: 8, core: 2. Of those that a mesh axis runs over, the one named last changes fastest.
Arguments:
- orbitals: bfloat16 [512, 2048, 128], P(('spin', 'dom')), parts along dimension 0, may hold values from -240 to 240
- potential: float32 [4096, 8, 128], P(('spin', 'dom')), parts along dimension 0, may hold values from -7 to 7
- cutoff: float32 [2], P('spin'), parts along dimension 0, may hold values from 3 to 9
- ceiling: float32 [2], P('spin'), parts along dimension 0, may hold values from 44 to 52
Outputs:
- rotated: bfloat16 [512, 2048, 128], P(('spin', 'dom')), parts along dimension 0
- projected: float32 [64, 32], P('spin'), parts along dimension 0
The draws below stay inside these ranges and needn't reach their ends.
There are 2 independent parts, one for each index of `spin`. The reference program is written for one: setup_inputs(seed, part) draws one part's arguments, and reference() takes and returns one part's arrays. A program takes and returns all parts, laid end to end along the dimension named above; each array names one. Nothing has to cross between parts.
All inputs are finite; a program needn't handle non-finite values.
Results may differ from the reference program's by a relative error of at most 0.0045.
Values may be sent and summed in bfloat16 or wider, within the bound.
No kernel may reach another device: no remote copies, remote signals or barrier semaphores. Data moves between devices by JAX's collectives and lax.ppermute only.
A program may use at most 64 MiB of HBM per device.

```python
import math
import jax
import jax.numpy as jnp
from jax import lax

NB = 32
NY = 8
NZ = 128
DEGREE = 3
NX = 2048


def draw_orbitals(key, part):
    key = jax.random.fold_in(key, 11)
    key_band, key_base = jax.random.split(key, 2)
    order = jax.random.permutation(key_band, NB).astype(jnp.float32)
    band_scale = jnp.exp(order * (math.log(10.0) / (NB - 1)))[:, None, None, None]
    places = jnp.arange(NX, dtype=jnp.float32)[None, None, :, None] / (NX - 1)
    shape = (NB, NY, NX, NZ)
    base = jnp.clip(jax.random.normal(key_base, shape, jnp.float32), -4.0, 4.0)
    envelope = jnp.exp(places * (0.5 * math.log(10.0)))
    return (base * band_scale * envelope).reshape(NB * NY, NX, NZ).astype(jnp.bfloat16)


def draw_potential(key, part):
    key = jax.random.fold_in(key, 23)
    key_freq, key_amp, key_phase, key_rough = jax.random.split(key, 4)
    freqs = jax.random.randint(key_freq, (4, 3), 1, 4).astype(jnp.float32)
    amplitudes = jax.random.uniform(key_amp, (4,), jnp.float32, 0.3, 0.8)
    phases = jax.random.uniform(key_phase, (4,), jnp.float32, -math.pi, math.pi)
    x_places = jnp.arange(NX, dtype=jnp.float32)[:, None, None] / NX
    y_places = jnp.arange(NY, dtype=jnp.float32)[None, :, None] / NY
    z_places = jnp.arange(NZ, dtype=jnp.float32)[None, None, :] / NZ
    smooth = jnp.zeros((NX, NY, NZ), jnp.float32)
    for mode in range(4):
        angle = 2.0 * math.pi * (freqs[mode, 0] * x_places + freqs[mode, 1] * y_places + freqs[mode, 2] * z_places)
        smooth = smooth + amplitudes[mode] * jnp.cos(angle + phases[mode])
    rough = 0.8 * jnp.clip(jax.random.normal(key_rough, (NX, NY, NZ), jnp.float32), -3.0, 3.0)
    return smooth + rough


def setup_inputs(seed: int = 0, part: int = 0) -> dict:
    seeds = jax.random.split(jax.random.key(seed), 5)
    part_keys = jax.random.split(jax.random.fold_in(seeds[4], part), 5)
    orbitals = draw_orbitals(jax.random.fold_in(jax.random.fold_in(seeds[4], part), 71), part)
    potential = draw_potential(jax.random.fold_in(jax.random.fold_in(seeds[4], part), 71), part)
    cutoff = jnp.clip(jax.random.uniform(part_keys[2], (1,), jnp.float32, 3.0, 9.0), 3.0, 9.0)
    ceiling = jnp.clip(jax.random.uniform(part_keys[3], (1,), jnp.float32, 44.0, 52.0), 44.0, 52.0)
    return dict(orbitals=orbitals, potential=potential, cutoff=cutoff, ceiling=ceiling)


STENCIL = (-5369.0 / 1800.0, 12.0 / 7.0, -15.0 / 56.0, 10.0 / 189.0, -1.0 / 112.0, 2.0 / 1925.0, -1.0 / 16632.0)
KINETIC = -2.0

def inner_products(left, right):
    return jnp.dot(left.astype(jnp.float32), right.T.astype(jnp.float32), precision=lax.Precision.HIGHEST, preferred_element_type=jnp.float32)

def apply_hamiltonian(field, potential_yx):
    y_cells, x_cells, z_cells = field.shape
    widened = jnp.pad(field, ((6, 6), (6, 6), (6, 6)))
    laplace = 3.0 * STENCIL[0] * field
    for offset in range(1, 7):
        weight = STENCIL[offset]
        upper = 6 + offset
        lower = 6 - offset
        laplace = laplace + weight * (widened[upper:upper + y_cells, 6:6 + x_cells, 6:6 + z_cells] + widened[lower:lower + y_cells, 6:6 + x_cells, 6:6 + z_cells])
        laplace = laplace + weight * (widened[6:6 + y_cells, upper:upper + x_cells, 6:6 + z_cells] + widened[6:6 + y_cells, lower:lower + x_cells, 6:6 + z_cells])
        laplace = laplace + weight * (widened[6:6 + y_cells, 6:6 + x_cells, upper:upper + z_cells] + widened[6:6 + y_cells, 6:6 + x_cells, lower:lower + z_cells])
    return KINETIC * laplace + potential_yx * field

def reference(orbitals, potential, cutoff, ceiling):
    fields = orbitals.reshape(NB, NY, NX, NZ).astype(jnp.float32)
    potential_yx = jnp.transpose(potential, (1, 0, 2))
    center = 0.5 * (ceiling[0] + cutoff[0])
    half_width = 0.5 * (ceiling[0] - cutoff[0])

    def filter_band(start):
        previous = start
        current = (apply_hamiltonian(start, potential_yx) - center * start) / half_width
        for repeat in range(DEGREE - 1):
            upcoming = 2.0 * (apply_hamiltonian(current, potential_yx) - center * current) / half_width - previous
            previous, current = (current, upcoming)
        return (current, apply_hamiltonian(current, potential_yx))
    filtered, ham_image = lax.map(filter_band, fields)
    cell_count = NX * NY * NZ
    flattened = filtered.reshape(NB, cell_count)
    gram_total = inner_products(flattened, flattened) / cell_count
    mixed_total = inner_products(flattened, ham_image.reshape(NB, cell_count)) / cell_count
    subspace_ham = 0.5 * (mixed_total + mixed_total.T)
    factor = jnp.linalg.cholesky(gram_total)
    inverse = jax.scipy.linalg.solve_triangular(factor, jnp.eye(NB, dtype=jnp.float32), lower=True)
    rotated = jnp.dot(inverse.astype(jnp.float32), flattened.astype(jnp.float32), precision=lax.Precision.HIGHEST, preferred_element_type=jnp.float32)
    rotated = rotated.astype(jnp.bfloat16).reshape(NB * NY, NX, NZ)
    left_part = jnp.dot(inverse.astype(jnp.float32), subspace_ham.astype(jnp.float32), precision=lax.Precision.HIGHEST, preferred_element_type=jnp.float32)
    projected = jnp.dot(left_part.astype(jnp.float32), inverse.T.astype(jnp.float32), precision=lax.Precision.HIGHEST, preferred_element_type=jnp.float32)
    return (rotated, projected)
```

```python
import jax
import jax.numpy as jnp
from jax import lax
from jax.sharding import Mesh, PartitionSpec as P

DEGREE = 3
DOM = ("x", "z", "y")


STENCIL = (
    -5369.0 / 1800.0,
    12.0 / 7.0,
    -15.0 / 56.0,
    10.0 / 189.0,
    -1.0 / 112.0,
    2.0 / 1925.0,
    -1.0 / 16632.0,
)
KINETIC = -2.0


def with_halo(cells, sides, width):
    for axis, dim in sides:
        count = lax.axis_size(axis)
        ends = count - 1
        head = lax.slice_in_dim(cells, 0, width, axis=dim).astype(jnp.bfloat16)
        tail = lax.slice_in_dim(cells, cells.shape[dim] - width, cells.shape[dim], axis=dim)
        tail = tail.astype(jnp.bfloat16)
        lower = lax.ppermute(tail, axis, [(i, (i + 1) % count) for i in range(ends)])
        upper = lax.ppermute(head, axis, [((i + 1) % count, i) for i in range(ends)])
        cells = jnp.concatenate(
            [lower.astype(cells.dtype), cells, upper.astype(cells.dtype)], axis=dim
        )
    return cells


def sum_over(value, axes):
    count = 1
    for axis in axes:
        count *= lax.axis_size(axis)
    copies = jnp.broadcast_to(value[None], (count,) + value.shape)
    return jnp.sum(lax.all_to_all(copies, axes, split_axis=0, concat_axis=0, tiled=True), axis=0)


def inner_products(left, right):
    return jnp.dot(
        left, right.T, precision=lax.Precision.HIGHEST, preferred_element_type=jnp.float32
    )


def stencil_apply(padded, potential_yx):
    band_count, y_cells, wide_planes, z_cells = padded.shape
    x_planes = wide_planes - 12
    field = padded[:, :, 6 : 6 + x_planes, :]
    widened = jnp.pad(field, ((0, 0), (6, 6), (0, 0), (6, 6)))
    laplace = 3.0 * STENCIL[0] * field
    for offset in range(1, 7):
        weight = STENCIL[offset]
        upper = 6 + offset
        lower = 6 - offset
        laplace = laplace + weight * (
            padded[:, :, upper : upper + x_planes, :] + padded[:, :, lower : lower + x_planes, :]
        )
        laplace = laplace + weight * (
            widened[:, upper : upper + y_cells, :, 6 : 6 + z_cells]
            + widened[:, lower : lower + y_cells, :, 6 : 6 + z_cells]
        )
        laplace = laplace + weight * (
            widened[:, 6 : 6 + y_cells, :, upper : upper + z_cells]
            + widened[:, 6 : 6 + y_cells, :, lower : lower + z_cells]
        )
    return KINETIC * laplace + potential_yx * field


def apply_hamiltonian(field, potential_yx):
    padded = with_halo(field, ((DOM, 2),), 6)
    return stencil_apply(padded, potential_yx)


def local(orbitals, potential, cutoff, ceiling):
    x_cells = orbitals.shape[1]
    z_cells = orbitals.shape[2]
    y_cells = potential.shape[1]
    slab_rows = lax.all_to_all(orbitals, DOM, split_axis=1, concat_axis=0, tiled=True)
    x_planes = slab_rows.shape[1]
    band_count = slab_rows.shape[0] // y_cells
    start = slab_rows.reshape(band_count, y_cells, x_planes, z_cells).astype(jnp.float32)
    potential_yx = jnp.swapaxes(potential, 0, 1)
    center = 0.5 * (ceiling[0] + cutoff[0])
    half_width = 0.5 * (ceiling[0] - cutoff[0])
    previous = start
    current = (apply_hamiltonian(start, potential_yx) - center * start) / half_width
    for repeat in range(DEGREE - 1):
        upcoming = (
            2.0 * (apply_hamiltonian(current, potential_yx) - center * current) / half_width
            - previous
        )
        previous, current = (current, upcoming)
    ham_image = None
    cell_count = x_cells * y_cells * z_cells
    flattened = current.reshape(band_count, y_cells * x_planes * z_cells)
    gram_part = inner_products(flattened, flattened)
    ham_image = apply_hamiltonian(current, potential_yx)
    mixed_part = inner_products(
        flattened, ham_image.reshape(band_count, y_cells * x_planes * z_cells)
    )
    totals = jnp.concatenate([gram_part, mixed_part], axis=0).reshape(16, 128)
    totals = sum_over(sum_over(totals, ("x", "y")), ("z",)).reshape(2 * band_count, band_count)
    gram_total, mixed_total = totals[:band_count], totals[band_count:]
    gram_total = gram_total / cell_count
    mixed_total = mixed_total / cell_count
    subspace_ham = 0.5 * (mixed_total + mixed_total.T)
    factor = jnp.linalg.cholesky(gram_total)
    inverse = jax.scipy.linalg.solve_triangular(
        factor, jnp.eye(band_count, dtype=jnp.float32), lower=True
    )
    rotated = jnp.dot(
        inverse, flattened, precision=lax.Precision.HIGHEST, preferred_element_type=jnp.float32
    )
    rotated = rotated.astype(jnp.bfloat16).reshape(band_count * y_cells, x_planes, z_cells)
    returned = lax.all_to_all(rotated, DOM, split_axis=0, concat_axis=1, tiled=True)
    left_part = jnp.dot(
        inverse, subspace_ham, precision=lax.Precision.HIGHEST, preferred_element_type=jnp.float32
    )
    projected = jnp.dot(
        left_part, inverse.T, precision=lax.Precision.HIGHEST, preferred_element_type=jnp.float32
    )
    return (returned, projected)


def solution(mesh):
    mesh = Mesh(mesh.devices.reshape(2, 4, 8, 4), ("spin",) + DOM)
    return jax.shard_map(
        local,
        mesh=mesh,
        in_specs=(
            P(("spin",) + DOM, None, None),
            P(("spin",) + DOM, None, None),
            P("spin"),
            P("spin"),
        ),
        out_specs=(P(("spin",) + DOM, None, None), P("spin", None)),
        check_vma=False,
    )
```

```python
import jax
import jax.numpy as jnp
import numpy as np
from jax import lax
from jax.experimental import pallas as pl
from jax.experimental.pallas import tpu as pltpu
from jax.sharding import Mesh, PartitionSpec as P

DOM = ("x", "z", "y")
BLOCKS = ("y", "z")

STENCIL = (
    -5369.0 / 1800.0,
    12.0 / 7.0,
    -15.0 / 56.0,
    10.0 / 189.0,
    -1.0 / 112.0,
    2.0 / 1925.0,
    -1.0 / 16632.0,
)
KINETIC = -2.0
SIDE = tuple(KINETIC * c for c in STENCIL[1:])
CENTRE = KINETIC * 3.0 * STENCIL[0]

NY = 8
NZ = 128
GROUP = 8
BANDS = 32
OWN = 64
HALO = 24
SPAN = OWN + 2 * HALO
SLAB = 16
AHEAD = 6
SENT = SLAB + AHEAD
ROWS = NY * GROUP
VMEM_LIMIT = 48 * 1024 * 1024


def split_bf16(value):
    high = value.astype(jnp.bfloat16)
    low = (value - high.astype(jnp.float32)).astype(jnp.bfloat16)
    return high, low


def z_matrix(sides):
    band = np.zeros((NZ, NZ), np.float64)
    for offset in range(1, 7):
        for cell in range(NZ - offset):
            band[cell + offset, cell] = SIDE[offset - 1]
            if sides == 2:
                band[cell, cell + offset] = SIDE[offset - 1]
    band = band.astype(np.float32)
    high = band.astype(jnp.bfloat16)
    low = (band - high.astype(np.float32)).astype(jnp.bfloat16)
    return high, low


def filter_kernel(
    scal, base, own, left, right, v_left, v_own, v_right, kz,
    out, own_f, left_f, right_f, u, s, y1, y2, y3,
):
    scale = scal[0]
    offset = scal[1]
    u[pl.ds(0, HALO * NY)] = (v_left[...] + offset) * scale
    u[pl.ds(HALO * NY, OWN * NY)] = (v_own[...] + offset) * scale
    u[pl.ds((HALO + OWN) * NY, HALO * NY)] = (v_right[...] + offset) * scale
    own_f[...] = own[...].astype(jnp.float32)
    left_f[...] = left[...].astype(jnp.float32)
    right_f[...] = right[...].astype(jnp.float32)

    def bring(source, planes, first):
        def step(x, carry):
            for y in range(NY):
                start = ((y // 2) * GROUP * 2 + y % 2) * planes + x
                s[first + x, pl.ds(y * GROUP, GROUP), :] = source[
                    pl.ds(start, GROUP, stride=2 * planes), :
                ]
            return carry

        lax.fori_loop(0, planes, step, 0, unroll=8)

    bring(left_f, HALO, 0)
    bring(own_f, OWN, HALO)
    bring(right_f, HALO, HALO + OWN)

    def level(source, source_first, before, before_first, target, first, last, start):
        def step(t, carry):
            i = first + 2 * t
            at = i - source_first
            block = source[pl.ds(at, 2)].reshape(2 * ROWS, NZ)
            if start:
                z = jnp.dot(
                    block.astype(jnp.bfloat16), kz[:NZ], preferred_element_type=jnp.float32
                )
            else:
                high, low = split_bf16(block)
                z = jnp.dot(
                    jnp.concatenate([high, low], axis=1), kz[...],
                    preferred_element_type=jnp.float32,
                )
            z = z[:, :NZ] + z[:, NZ:]
            for p in range(2):
                plane = base[0] + i + p
                inside = (plane >= 0) & (plane < base[1])
                factor = jnp.where(inside, scale, 0.0)
                cells = [block[p * ROWS + y * GROUP : p * ROWS + (y + 1) * GROUP] for y in range(NY)]
                for y in range(NY):
                    here = pl.ds(y * GROUP, GROUP)
                    total = z[p * ROWS + y * GROUP : p * ROWS + (y + 1) * GROUP]
                    for k in range(1, 7):
                        pair = source[at + p + k, here, :] + source[at + p - k, here, :]
                        if y + k < NY:
                            pair = pair + cells[y + k]
                        if y - k >= 0:
                            pair = pair + cells[y - k]
                        total = total + SIDE[k - 1] * pair
                    local = jnp.broadcast_to(u[pl.ds((i + p) * NY + y, 1), :], (GROUP, NZ))
                    value = factor * total + local * cells[y]
                    if start:
                        value = 0.5 * value
                    else:
                        value = value - before[i + p - before_first, here, :]
                    target[i + p - first, here, :] = value
            return carry

        lax.fori_loop(0, (last - first) // 2, step, 0)

    level(s, 0, None, 0, y1, 12, 106, True)
    level(y1, 12, s, 0, y2, 18, 100, False)
    level(y2, 18, y1, 12, y3, 24, 94, False)
    for dest in range(OWN // SLAB):
        out[dest] = y3[pl.ds(dest * SLAB, SENT)].astype(jnp.bfloat16)


def filtered_planes(scal, base, own, left, right, v_left, v_own, v_right):
    high, low = z_matrix(2)
    zero = np.zeros_like(high)
    kz = jnp.asarray(np.block([[high, low], [high, zero]]))
    smem = pl.BlockSpec(memory_space=pltpu.SMEM)
    vmem = pl.BlockSpec(memory_space=pltpu.VMEM)
    f32 = jnp.float32
    return pl.pallas_call(
        filter_kernel,
        out_shape=jax.ShapeDtypeStruct((OWN // SLAB, SENT, ROWS, NZ), jnp.bfloat16),
        in_specs=[smem, smem] + [vmem] * 7,
        out_specs=vmem,
        scratch_shapes=[
            pltpu.VMEM((ROWS * OWN, NZ), f32),
            pltpu.VMEM((ROWS * HALO, NZ), f32),
            pltpu.VMEM((ROWS * HALO, NZ), f32),
            pltpu.VMEM((SPAN * NY, NZ), f32),
            pltpu.VMEM((SPAN, ROWS, NZ), f32),
            pltpu.VMEM((94, ROWS, NZ), f32),
            pltpu.VMEM((82, ROWS, NZ), f32),
            pltpu.VMEM((70, ROWS, NZ), f32),
        ],
        compiler_params=pltpu.CompilerParams(vmem_limit_bytes=VMEM_LIMIT),
        name="filter_planes",
    )(scal, base, own, left, right, v_left, v_own, v_right, kz)


def sums_kernel(planes, v, kz, out, cells_f, total):
    def unpack(x, carry):
        for g in range(BANDS // GROUP):
            part = planes[g, x].astype(jnp.float32).reshape(NY, GROUP, NZ)
            cells_f[x, :, pl.ds(g * GROUP, GROUP), :] = part
        return carry

    lax.fori_loop(0, SENT, unpack, 0)
    total[...] = jnp.zeros_like(total)

    def step(x, carry):
        block = cells_f[x].reshape(NY * BANDS, NZ)
        block16 = block.astype(jnp.bfloat16)
        z = jnp.dot(block16, kz[...], preferred_element_type=jnp.float32)
        z = z[:, :NZ] + z[:, NZ:]
        cells = [block[y * BANDS : (y + 1) * BANDS] for y in range(NY)]
        cells16 = [block16[y * BANDS : (y + 1) * BANDS] for y in range(NY)]
        images = []
        for y in range(NY):
            image = z[y * BANDS : (y + 1) * BANDS]
            for k in range(1, 7):
                pair = cells_f[x + k, y]
                if y + k < NY:
                    pair = pair + cells[y + k]
                image = image + SIDE[k - 1] * pair
            local = jnp.broadcast_to(v[x, pl.ds(y, 1), :], (BANDS, NZ))
            image = image + (0.5 * (local + CENTRE)) * cells[y]
            images.append(image)
        add = total[...]
        for y in range(0, NY, 2):
            first = split_bf16(images[y])
            second = split_bf16(images[y + 1])
            lhs = jnp.concatenate([cells16[y], cells16[y + 1]], axis=1)
            rhs = jnp.concatenate(
                [
                    lhs,
                    jnp.concatenate([first[0], second[0]], axis=1),
                    jnp.concatenate([first[1], second[1]], axis=1),
                ],
                axis=0,
            )
            add = add + lax.dot_general(
                lhs, rhs, (((1,), (1,)), ((), ())), preferred_element_type=jnp.float32
            )
        total[...] = add
        return carry

    lax.fori_loop(0, SLAB, step, 0)
    sums = total[...]
    gram = sums[:, :BANDS]
    half = sums[:, BANDS : 2 * BANDS] + sums[:, 2 * BANDS :]
    both = jnp.concatenate([gram, half], axis=1)
    row = jnp.concatenate([both[:16], both[16:]], axis=1)
    for copy in range(out.shape[0]):
        out[copy] = row


def matrix_sums(planes, v, copies):
    kz = jnp.asarray(np.concatenate(z_matrix(1), axis=1))
    vmem = pl.BlockSpec(memory_space=pltpu.VMEM)
    f32 = jnp.float32
    return pl.pallas_call(
        sums_kernel,
        out_shape=jax.ShapeDtypeStruct((copies, 16, NZ), f32),
        in_specs=[vmem] * 3,
        out_specs=vmem,
        scratch_shapes=[
            pltpu.VMEM((SENT, NY, BANDS, NZ), f32),
            pltpu.VMEM((BANDS, 3 * BANDS), f32),
        ],
        compiler_params=pltpu.CompilerParams(vmem_limit_bytes=VMEM_LIMIT),
        name="matrix_sums",
    )(planes, v, kz)


def rotate_kernel(count, parts, planes, out, projected, turned):
    sums = jnp.sum(parts[...], axis=0) * (1.0 / count)
    gram = jnp.concatenate([sums[:, :32], sums[:, 64:96]], axis=0)
    half = jnp.concatenate([sums[:, 32:64], sums[:, 96:]], axis=0)
    ham = half + half.T
    rows = lax.broadcasted_iota(jnp.int32, (BANDS, BANDS), 0)
    columns = lax.broadcasted_iota(jnp.int32, (BANDS, BANDS), 1)
    unit = jnp.where(rows == columns, 1.0, 0.0).astype(jnp.float32)
    work = jnp.concatenate([gram, unit], axis=1)
    index = lax.broadcasted_iota(jnp.int32, (BANDS, 1), 0)
    for k in range(BANDS):
        pivot = work[k : k + 1, k : k + 1]
        row = work[k : k + 1] / jnp.sqrt(pivot)
        lower = jnp.where(index > k, work[:, k : k + 1] / jnp.sqrt(pivot), 0.0)
        work = jnp.where(index == k, row, work - lower * row)
    inverse = work[:, BANDS:]
    high = lax.Precision.HIGHEST
    left = jnp.dot(inverse, ham, precision=high, preferred_element_type=jnp.float32)
    projected[...] = lax.dot_general(
        left, inverse, (((1,), (1,)), ((), ())), precision=high,
        preferred_element_type=jnp.float32,
    )
    both = jnp.concatenate(split_bf16(inverse), axis=1)

    def turn(x, carry):
        parts32 = [planes[g, x].astype(jnp.float32) for g in range(BANDS // GROUP)]
        wide = []
        for y in range(NY):
            wide.append(
                jnp.concatenate([p[y * GROUP : (y + 1) * GROUP] for p in parts32], axis=0)
            )
        data = jnp.concatenate(wide, axis=1).astype(jnp.bfloat16)
        data = jnp.concatenate([data, data], axis=0)
        result = jnp.dot(both, data, preferred_element_type=jnp.float32)
        for y in range(NY):
            start = pl.multiple_of((x * NY + y) * BANDS, BANDS)
            turned[pl.ds(start, BANDS), :] = result[:, y * NZ : (y + 1) * NZ]
        return carry

    lax.fori_loop(0, SLAB, turn, 0)

    def give(b, carry):
        for pair in range(NY // 2):
            for g in range(BANDS // GROUP):
                for odd in range(2):
                    start = (2 * pair + odd) * BANDS + g * GROUP + b
                    value = turned[pl.ds(start, SLAB, stride=NY * BANDS), :]
                    out[(pair * GROUP + b) * (BANDS // GROUP) + g, odd] = value.astype(jnp.bfloat16)
        return carry

    lax.fori_loop(0, GROUP, give, 0)


def rotated_planes(parts, planes, count):
    vmem = pl.BlockSpec(memory_space=pltpu.VMEM)

    def kernel(*refs):
        rotate_kernel(count, *refs)

    return pl.pallas_call(
        kernel,
        out_shape=(
            jax.ShapeDtypeStruct((128, 2, SLAB, NZ), jnp.bfloat16),
            jax.ShapeDtypeStruct((BANDS, BANDS), jnp.float32),
        ),
        in_specs=[vmem] * 2,
        out_specs=(vmem, vmem),
        scratch_shapes=[pltpu.VMEM((SLAB * NY * BANDS, NZ), jnp.float32)],
        compiler_params=pltpu.CompilerParams(vmem_limit_bytes=VMEM_LIMIT),
        name="rotate_planes",
    )(parts, planes)


def local(orbitals, potential, cutoff, ceiling):
    x_cells = orbitals.shape[1]
    block_count = x_cells // OWN
    center = 0.5 * (ceiling[0] + cutoff[0])
    half_width = 0.5 * (ceiling[0] - cutoff[0])
    scal = jnp.stack([2.0 / half_width, CENTRE - center])
    block_index = lax.axis_index(BLOCKS)
    base = jnp.stack([block_index * OWN - HALO, jnp.int32(x_cells)])
    place = [z * 4 + y for y in range(4) for z in range(8)]
    up = [(place[i], place[i + 1]) for i in range(block_count - 1)]
    down = [(b, a) for a, b in up]

    swap = [(a * 4 + b, b * 4 + a) for a in range(4) for b in range(4)]
    v_slab = lax.ppermute(potential, ("x", "y"), swap)
    v_own = lax.all_gather(v_slab, "x", tiled=True)
    v_left = lax.ppermute(v_own[OWN - HALO :], ("z", "y"), up)
    v_right = lax.ppermute(v_own[:HALO], ("z", "y"), down)

    chunks = orbitals.reshape(2, block_count, OWN, NZ).swapaxes(0, 1)
    own = lax.all_to_all(chunks, BLOCKS, split_axis=0, concat_axis=0, tiled=True)
    left = lax.ppermute(own[:, :, OWN - HALO :].reshape(ROWS * HALO, NZ), ("z", "y"), up)
    right = lax.ppermute(own[:, :, :HALO].reshape(ROWS * HALO, NZ), ("z", "y"), down)
    filtered = filtered_planes(
        scal,
        base,
        own.reshape(ROWS * OWN, NZ),
        left,
        right,
        v_left.reshape(HALO * NY, NZ),
        v_own.reshape(OWN * NY, NZ),
        v_right.reshape(HALO * NY, NZ),
    )
    planes = lax.all_to_all(filtered, "x", split_axis=0, concat_axis=0, tiled=True)
    sums = matrix_sums(planes, v_slab, 16)
    sums = lax.all_to_all(sums, ("x", "y"), split_axis=0, concat_axis=0, tiled=True)
    sums = jnp.broadcast_to(jnp.sum(sums, axis=0)[None], (8, 16, NZ))
    sums = lax.all_to_all(sums, "z", split_axis=0, concat_axis=0, tiled=True)
    rotated, projected = rotated_planes(sums, planes, x_cells * NY * NZ)
    returned = lax.all_to_all(rotated, ("y", "z", "x"), split_axis=0, concat_axis=0, tiled=True)
    returned = returned.swapaxes(0, 1).reshape(2, x_cells, NZ)
    return (returned, projected)


def solution(mesh):
    mesh = Mesh(mesh.devices.reshape(2, 4, 8, 4), ("spin",) + DOM)
    return jax.shard_map(
        local,
        mesh=mesh,
        in_specs=(
            P(("spin",) + DOM, None, None),
            P(("spin",) + DOM, None, None),
            P("spin"),
            P("spin"),
        ),
        out_specs=(P(("spin",) + DOM, None, None), P("spin", None)),
        check_vma=False,
    )
```

```python
import jax
import jax.numpy as jnp
import numpy as np
from jax import lax
from jax.experimental import pallas as pl
from jax.experimental.pallas import tpu as pltpu
from jax.sharding import Mesh, PartitionSpec as P

DOM = ("x", "z", "y")
BLOCKS = ("y", "z")

STENCIL = (
    -5369.0 / 1800.0,
    12.0 / 7.0,
    -15.0 / 56.0,
    10.0 / 189.0,
    -1.0 / 112.0,
    2.0 / 1925.0,
    -1.0 / 16632.0,
)
KINETIC = -2.0
SIDE = tuple(KINETIC * c for c in STENCIL[1:])
CENTRE = KINETIC * 3.0 * STENCIL[0]

NY = 8
NZ = 128
GROUP = 8
BANDS = 32
OWN = 64
HALO = 24
SPAN = OWN + 2 * HALO
SLAB = 16
AHEAD = 6
SENT = SLAB + AHEAD
ROWS = NY * GROUP
EDGE = 12
PLANES = 8
VMEM_LIMIT = 48 * 1024 * 1024


def split_bf16(value):
    high = value.astype(jnp.bfloat16)
    low = (value - high.astype(jnp.float32)).astype(jnp.bfloat16)
    return high, low


def z_matrix(sides):
    band = np.zeros((NZ, NZ), np.float64)
    for offset in range(1, 7):
        for cell in range(NZ - offset):
            band[cell + offset, cell] = SIDE[offset - 1]
            if sides == 2:
                band[cell, cell + offset] = SIDE[offset - 1]
    band = band.astype(np.float32)
    high = band.astype(jnp.bfloat16)
    low = (band - high.astype(np.float32)).astype(jnp.bfloat16)
    return high, low


def level(
    kz, u, scale, base, source, source_first, before, before_first,
    target, target_first, first, last, count, start=False,
):
    def step(t, carry):
        i = first + count * t
        at = i - source_first
        block = source[pl.ds(at, count)].reshape(count * ROWS, NZ)
        if start:
            z = jnp.dot(block.astype(jnp.bfloat16), kz[:NZ], preferred_element_type=jnp.float32)
        else:
            z = jnp.dot(
                jnp.concatenate(split_bf16(block), axis=1), kz[...],
                preferred_element_type=jnp.float32,
            )
        for p in range(count):
            factor = scale
            if base is not None:
                plane = base[0] + i + p
                factor = jnp.where((plane >= 0) & (plane < base[1]), scale, 0.0)
            at_y = [slice(p * ROWS + y * GROUP, p * ROWS + (y + 1) * GROUP) for y in range(NY)]
            for y in range(NY):
                here = pl.ds(y * GROUP, GROUP)
                total = None
                for k in range(1, 7):
                    pair = source[at + p + k, here, :] + source[at + p - k, here, :]
                    if y + k < NY:
                        pair = pair + block[at_y[y + k]]
                    if y - k >= 0:
                        pair = pair + block[at_y[y - k]]
                    pair = SIDE[k - 1] * pair
                    total = pair if total is None else total + pair
                total = total + (z[at_y[y], :NZ] + z[at_y[y], NZ:])
                local = jnp.broadcast_to(u[pl.ds((i + p) * NY + y, 1), :], (GROUP, NZ))
                value = factor * total + local * block[at_y[y]]
                if start:
                    value = 0.5 * value
                else:
                    value = value - before[i + p - before_first, here, :]
                target[i + p - target_first, here, :] = value
        return carry

    lax.fori_loop(0, (last - first) // count, step, 0)


def bring(source, planes, target, first):
    def step(x, carry):
        for y in range(NY):
            start = ((y // 2) * GROUP * 2 + y % 2) * planes + x
            target[first + x, pl.ds(y * GROUP, GROUP), :] = source[
                pl.ds(start, GROUP, stride=2 * planes), :
            ]
        return carry

    lax.fori_loop(0, planes, step, 0, unroll=8)


def inner_kernel(scal, own, v_own, kz, s_edge, y1_edge, y2_edge, y3_inner, own_f, u, s, y1, y2, y3):
    scale = scal[0]
    u[pl.ds(HALO * NY, OWN * NY)] = (v_own[...] + scal[1]) * scale
    own_f[...] = own[...].astype(jnp.float32)
    bring(own_f, OWN, s, 0)
    level(kz, u, scale, None, s, 24, None, 0, y1, 30, 30, 82, 13, start=True)
    level(kz, u, scale, None, y1, 30, s, 24, y2, 36, 36, 76, 10)
    level(kz, u, scale, None, y2, 36, y1, 30, y3, 42, 42, 70, 14)
    for ref, edge in ((s, s_edge), (y1, y1_edge), (y2, y2_edge)):
        edge[0] = ref[pl.ds(0, EDGE)]
        edge[1] = ref[pl.ds(ref.shape[0] - EDGE, EDGE)]
    y3_inner[...] = y3[...].astype(jnp.bfloat16)


def outer_kernel(
    scal, base, left, right, v_own, s_edge, y1_edge, y2_edge, y3_inner, kz,
    out, side_f, u, s, y1, y2, y3,
):
    scale = scal[0]
    v_rows = HALO * NY
    u[pl.ds(v_rows, OWN * NY)] = (v_own[...] + scal[1]) * scale
    y3[pl.ds(18, 28)] = y3_inner[...].astype(jnp.float32)
    for side, halo in ((0, left), (1, right)):
        field_rows = ROWS * HALO
        side_f[...] = halo[...].astype(jnp.float32)
        v = side_f[pl.ds(field_rows, v_rows)] + side_f[pl.ds(field_rows + v_rows, v_rows)]
        u[pl.ds(side * (HALO + OWN) * NY, v_rows)] = (v + scal[1]) * scale
        halo_at, edge_at = ((0, HALO), (EDGE, 0))[side]
        bring(side_f, HALO, s, halo_at)
        s[pl.ds(edge_at, EDGE)] = s_edge[side]
        y1_at, y2_at = ((18, 18), (0, 0))[side]
        y1[pl.ds(y1_at, EDGE)] = y1_edge[side]
        y2[pl.ds(y2_at, EDGE)] = y2_edge[side]
        if side == 0:
            level(kz, u, scale, base, s, 0, None, 0, y1, 12, 12, 30, 9, start=True)
            level(kz, u, scale, base, y1, 12, s, 0, y2, 18, 18, 36, 9)
            level(kz, u, scale, base, y2, 18, y1, 12, y3, 24, 24, 42, 9)
        else:
            level(kz, u, scale, base, s, 76, None, 0, y1, 70, 82, 106, 12, start=True)
            level(kz, u, scale, base, y1, 70, s, 76, y2, 64, 76, 100, 12)
            level(kz, u, scale, base, y2, 64, y1, 70, y3, 24, 70, 94, 12)
    for dest in range(OWN // SLAB):
        out[dest] = y3[pl.ds(dest * SLAB, SENT)].astype(jnp.bfloat16)


def z_both():
    high, low = z_matrix(2)
    return jnp.asarray(np.block([[high, low], [high, np.zeros_like(high)]]))


def inner_planes(scal, own, v_own):
    smem = pl.BlockSpec(memory_space=pltpu.SMEM)
    vmem = pl.BlockSpec(memory_space=pltpu.VMEM)
    f32 = jnp.float32
    edge = jax.ShapeDtypeStruct((2, EDGE, ROWS, NZ), f32)
    return pl.pallas_call(
        inner_kernel,
        out_shape=(edge, edge, edge, jax.ShapeDtypeStruct((28, ROWS, NZ), jnp.bfloat16)),
        in_specs=[smem] + [vmem] * 3,
        out_specs=[vmem] * 4,
        scratch_shapes=[
            pltpu.VMEM((ROWS * OWN, NZ), f32),
            pltpu.VMEM((SPAN * NY, NZ), f32),
            pltpu.VMEM((64, ROWS, NZ), f32),
            pltpu.VMEM((52, ROWS, NZ), f32),
            pltpu.VMEM((40, ROWS, NZ), f32),
            pltpu.VMEM((28, ROWS, NZ), f32),
        ],
        compiler_params=pltpu.CompilerParams(vmem_limit_bytes=VMEM_LIMIT),
        cost_estimate=pl.CostEstimate(
            flops=2_000_000_000, bytes_accessed=8_000_000, transcendentals=0
        ),
        name="filter_inner",
    )(scal, own, v_own, z_both())


def outer_planes(scal, base, left, right, v_own, inner):
    smem = pl.BlockSpec(memory_space=pltpu.SMEM)
    vmem = pl.BlockSpec(memory_space=pltpu.VMEM)
    f32 = jnp.float32
    return pl.pallas_call(
        outer_kernel,
        out_shape=jax.ShapeDtypeStruct((OWN // SLAB, SENT, ROWS, NZ), jnp.bfloat16),
        in_specs=[smem, smem] + [vmem] * 8,
        out_specs=vmem,
        scratch_shapes=[
            pltpu.VMEM(left.shape, f32),
            pltpu.VMEM((SPAN * NY, NZ), f32),
            pltpu.VMEM((36, ROWS, NZ), f32),
            pltpu.VMEM((36, ROWS, NZ), f32),
            pltpu.VMEM((36, ROWS, NZ), f32),
            pltpu.VMEM((70, ROWS, NZ), f32),
        ],
        compiler_params=pltpu.CompilerParams(vmem_limit_bytes=VMEM_LIMIT),
        name="filter_outer",
    )(scal, base, left, right, v_own, *inner, z_both())


def sums_kernel(planes, v, kz, out, fields_out, cells_f, total):
    def unpack(x, carry):
        for g in range(BANDS // GROUP):
            part = planes[g, x].astype(jnp.float32).reshape(NY, GROUP, NZ)
            cells_f[x, :, pl.ds(g * GROUP, GROUP), :] = part
        return carry

    lax.fori_loop(0, SENT, unpack, 0)
    total[...] = jnp.zeros_like(total)

    def step(t, carry):
        x0 = t * PLANES
        block = cells_f[pl.ds(x0, PLANES)].reshape(PLANES * NY * BANDS, NZ)
        block16 = block.astype(jnp.bfloat16)
        z = jnp.dot(block16, kz[...], preferred_element_type=jnp.float32)
        add = total[...]
        for p in range(PLANES):
            x = x0 + p
            at = [slice((p * NY + y) * BANDS, (p * NY + y + 1) * BANDS) for y in range(NY)]
            images = []
            for y in range(NY):
                image = None
                for k in range(1, 7):
                    pair = cells_f[x + k, y]
                    if y + k < NY:
                        pair = pair + block[at[y + k]]
                    pair = SIDE[k - 1] * pair
                    image = pair if image is None else image + pair
                local = jnp.broadcast_to(v[x, pl.ds(y, 1), :], (BANDS, NZ))
                image = image + (0.5 * (local + CENTRE)) * block[at[y]]
                images.append(split_bf16(image + (z[at[y], :NZ] + z[at[y], NZ:])))
            fields = jnp.concatenate([block16[a] for a in at], axis=1)
            fields_out[x] = fields
            highs = jnp.concatenate([i[0] for i in images], axis=1)
            lows = jnp.concatenate([i[1] for i in images], axis=1)
            add = add + lax.dot_general(
                jnp.concatenate([fields, highs, lows], axis=0), fields,
                (((1,), (1,)), ((), ())), preferred_element_type=jnp.float32,
            )
        total[...] = add
        return carry

    lax.fori_loop(0, SLAB // PLANES, step, 0)
    sums = total[...]
    gram = sums[:BANDS]
    half = sums[BANDS : 2 * BANDS] + sums[2 * BANDS :]
    both = jnp.concatenate([gram, half], axis=1)
    row = jnp.concatenate([both[:16], both[16:]], axis=1)
    for copy in range(out.shape[0]):
        out[copy] = row


def matrix_sums(planes, v, copies):
    kz = jnp.asarray(np.concatenate(z_matrix(1), axis=1))
    vmem = pl.BlockSpec(memory_space=pltpu.VMEM)
    f32 = jnp.float32
    return pl.pallas_call(
        sums_kernel,
        out_shape=(
            jax.ShapeDtypeStruct((copies, 16, NZ), f32),
            jax.ShapeDtypeStruct((SLAB, BANDS, NY * NZ), jnp.bfloat16),
        ),
        in_specs=[vmem] * 3,
        out_specs=(vmem, vmem),
        scratch_shapes=[
            pltpu.VMEM((SENT, NY, BANDS, NZ), f32),
            pltpu.VMEM((3 * BANDS, BANDS), f32),
        ],
        compiler_params=pltpu.CompilerParams(vmem_limit_bytes=VMEM_LIMIT),
        name="matrix_sums",
    )(planes, v, kz)


def rotate_kernel(count, parts, fields, out, projected, turned):
    sums = jnp.sum(parts[...], axis=0) * (1.0 / count)
    gram = jnp.concatenate([sums[:, :32], sums[:, 64:96]], axis=0)
    half = jnp.concatenate([sums[:, 32:64], sums[:, 96:]], axis=0)
    ham = half + half.T
    rows = lax.broadcasted_iota(jnp.int32, (BANDS, BANDS), 0)
    columns = lax.broadcasted_iota(jnp.int32, (BANDS, BANDS), 1)
    unit = jnp.where(rows == columns, 1.0, 0.0).astype(jnp.float32)
    work = jnp.concatenate([gram, unit], axis=1)
    index = lax.broadcasted_iota(jnp.int32, (BANDS, 1), 0)
    def column(k):
        return jnp.broadcast_to(work[:, k : k + 1], (BANDS, 2 * BANDS))

    now, after = column(0), column(1)
    for k in range(BANDS):
        inverse_pivot = 1.0 / now[k : k + 1]
        lower = jnp.where(index > k, now, 0.0)
        work = work - lower * (work[k : k + 1] * inverse_pivot)
        if k + 1 < BANDS:
            now = after - lower * (after[k : k + 1] * inverse_pivot)
        if k + 2 < BANDS:
            after = column(k + 2)
    pivots = jnp.sum(jnp.where(rows == columns, work[:, :BANDS], 0.0), axis=1, keepdims=True)
    inverse = work[:, BANDS:] / jnp.sqrt(pivots)
    high = lax.Precision.HIGHEST
    left = jnp.dot(inverse, ham, precision=high, preferred_element_type=jnp.float32)
    projected[...] = lax.dot_general(
        left, inverse, (((1,), (1,)), ((), ())), precision=high,
        preferred_element_type=jnp.float32,
    )
    both = jnp.concatenate(split_bf16(inverse), axis=1)

    def turn(x, carry):
        data = fields[x]
        data = jnp.concatenate([data, data], axis=0)
        result = jnp.dot(both, data, preferred_element_type=jnp.float32)
        for y in range(NY):
            start = pl.multiple_of((x * NY + y) * BANDS, BANDS)
            turned[pl.ds(start, BANDS), :] = result[:, y * NZ : (y + 1) * NZ]
        return carry

    lax.fori_loop(0, SLAB, turn, 0)

    def give(b, carry):
        for pair in range(NY // 2):
            for g in range(BANDS // GROUP):
                for odd in range(2):
                    start = (2 * pair + odd) * BANDS + g * GROUP + b
                    value = turned[pl.ds(start, SLAB, stride=NY * BANDS), :]
                    out[(pair * GROUP + b) * (BANDS // GROUP) + g, odd] = value.astype(jnp.bfloat16)
        return carry

    lax.fori_loop(0, GROUP, give, 0)


def rotated_planes(parts, fields, count):
    vmem = pl.BlockSpec(memory_space=pltpu.VMEM)

    def kernel(*refs):
        rotate_kernel(count, *refs)

    return pl.pallas_call(
        kernel,
        out_shape=(
            jax.ShapeDtypeStruct((128, 2, SLAB, NZ), jnp.bfloat16),
            jax.ShapeDtypeStruct((BANDS, BANDS), jnp.float32),
        ),
        in_specs=[vmem] * 2,
        out_specs=(vmem, vmem),
        scratch_shapes=[pltpu.VMEM((SLAB * NY * BANDS, NZ), jnp.float32)],
        compiler_params=pltpu.CompilerParams(vmem_limit_bytes=VMEM_LIMIT),
        name="rotate_planes",
    )(parts, fields)


def local(orbitals, potential, cutoff, ceiling):
    x_cells = orbitals.shape[1]
    block_count = x_cells // OWN
    center = 0.5 * (ceiling[0] + cutoff[0])
    half_width = 0.5 * (ceiling[0] - cutoff[0])
    scal = jnp.stack([2.0 / half_width, CENTRE - center])
    block_index = lax.axis_index(BLOCKS)
    base = jnp.stack([block_index * OWN - HALO, jnp.int32(x_cells)])
    place = [z * 4 + y for y in range(4) for z in range(8)]
    up = [(place[i], place[i + 1]) for i in range(block_count - 1)]
    down = [(b, a) for a, b in up]

    x_index = lax.axis_index("x")
    slabs = [
        lax.ppermute(
            potential,
            ("x", "y"),
            [(y * 4 + (x + j) % 4, x * 4 + y) for x in range(4) for y in range(4)],
        )
        for j in range(4)
    ]
    v_slab = slabs[0]
    v_own = lax.dynamic_slice_in_dim(
        jnp.concatenate(slabs[1:] + slabs), (3 - x_index) * SLAB, OWN, axis=0
    )

    chunks = orbitals.reshape(2, block_count, OWN, NZ).swapaxes(0, 1)
    own = lax.all_to_all(chunks, BLOCKS, split_axis=0, concat_axis=0, tiled=True)
    def with_potential(field, v):
        parts = [p.reshape(HALO * NY, NZ) for p in split_bf16(v)]
        return jnp.concatenate([field.reshape(ROWS * HALO, NZ)] + parts, axis=0)

    tail = with_potential(own[:, :, OWN - HALO :], v_own[OWN - HALO :])
    head = with_potential(own[:, :, :HALO], v_own[:HALO])
    left = lax.ppermute(tail, ("z", "y"), up)
    right = lax.ppermute(head, ("z", "y"), down)
    v_rows = v_own.reshape(OWN * NY, NZ)
    inner = inner_planes(scal, own.reshape(ROWS * OWN, NZ), v_rows)
    filtered = outer_planes(scal, base, left, right, v_rows, inner)
    planes = lax.all_to_all(filtered, "x", split_axis=0, concat_axis=0, tiled=True)
    sums, fields = matrix_sums(planes, v_slab, 16)
    sums = lax.all_to_all(sums, ("x", "y"), split_axis=0, concat_axis=0, tiled=True)
    sums = jnp.broadcast_to(jnp.sum(sums, axis=0)[None], (8, 16, NZ))
    sums = lax.all_to_all(sums, "z", split_axis=0, concat_axis=0, tiled=True)
    rotated, projected = rotated_planes(sums, fields, x_cells * NY * NZ)
    returned = lax.all_to_all(rotated, ("y", "z", "x"), split_axis=0, concat_axis=0, tiled=True)
    returned = returned.swapaxes(0, 1).reshape(2, x_cells, NZ)
    return (returned, projected)


def solution(mesh):
    mesh = Mesh(mesh.devices.reshape(2, 4, 8, 4), ("spin",) + DOM)
    return jax.shard_map(
        local,
        mesh=mesh,
        in_specs=(
            P(("spin",) + DOM, None, None),
            P(("spin",) + DOM, None, None),
            P("spin"),
            P("spin"),
        ),
        out_specs=(P(("spin",) + DOM, None, None), P("spin", None)),
        check_vma=False,
    )
```

```python
import jax
import jax.numpy as jnp
import numpy as np
from jax import lax
from jax.experimental import pallas as pl
from jax.experimental.pallas import tpu as pltpu
from jax.sharding import Mesh, PartitionSpec as P

DOM = ("x", "h", "l", "y")
BLOCKS = ("y", "h", "l")

STENCIL = (
    -5369.0 / 1800.0,
    12.0 / 7.0,
    -15.0 / 56.0,
    10.0 / 189.0,
    -1.0 / 112.0,
    2.0 / 1925.0,
    -1.0 / 16632.0,
)
KINETIC = -2.0
SIDE = tuple(KINETIC * c for c in STENCIL[1:])
CENTRE = KINETIC * 3.0 * STENCIL[0]

NY = 8
NZ = 128
GROUP = 8
BANDS = 32
OWN = 64
HALO = 24
SPAN = OWN + 2 * HALO
SLAB = 16
AHEAD = 6
SENT = SLAB + AHEAD
ROWS = NY * GROUP
EDGE = 12
PLANES = 8
VMEM_LIMIT = 48 * 1024 * 1024


def split_bf16(value):
    high = value.astype(jnp.bfloat16)
    low = (value - high.astype(jnp.float32)).astype(jnp.bfloat16)
    return high, low


def z_matrix(sides):
    band = np.zeros((NZ, NZ), np.float64)
    for offset in range(1, 7):
        for cell in range(NZ - offset):
            band[cell + offset, cell] = SIDE[offset - 1]
            if sides == 2:
                band[cell, cell + offset] = SIDE[offset - 1]
    band = band.astype(np.float32)
    high = band.astype(jnp.bfloat16)
    low = (band - high.astype(np.float32)).astype(jnp.bfloat16)
    return high, low


def level(
    kz, u, scale, base, source, source_first, before, before_first,
    target, target_first, first, last, count, start=False,
):
    def step(t, carry):
        i = first + count * t
        at = i - source_first
        block = source[pl.ds(at, count)].reshape(count * ROWS, NZ)
        if start:
            z = jnp.dot(block.astype(jnp.bfloat16), kz[:NZ], preferred_element_type=jnp.float32)
        else:
            z = jnp.dot(
                jnp.concatenate(split_bf16(block), axis=1), kz[...],
                preferred_element_type=jnp.float32,
            )
        for p in range(count):
            factor = scale
            if base is not None:
                plane = base[0] + i + p
                factor = jnp.where((plane >= 0) & (plane < base[1]), scale, 0.0)
            at_y = [slice(p * ROWS + y * GROUP, p * ROWS + (y + 1) * GROUP) for y in range(NY)]
            for y in range(NY):
                here = pl.ds(y * GROUP, GROUP)
                total = None
                for k in range(1, 7):
                    pair = source[at + p + k, here, :] + source[at + p - k, here, :]
                    if y + k < NY:
                        pair = pair + block[at_y[y + k]]
                    if y - k >= 0:
                        pair = pair + block[at_y[y - k]]
                    pair = SIDE[k - 1] * pair
                    total = pair if total is None else total + pair
                total = total + (z[at_y[y], :NZ] + z[at_y[y], NZ:])
                local = jnp.broadcast_to(u[pl.ds((i + p) * NY + y, 1), :], (GROUP, NZ))
                value = factor * total + local * block[at_y[y]]
                if start:
                    value = 0.5 * value
                else:
                    value = value - before[i + p - before_first, here, :]
                target[i + p - target_first, here, :] = value
        return carry

    lax.fori_loop(0, (last - first) // count, step, 0)


def bring(source, planes, target, first):
    def step(x, carry):
        for y in range(NY):
            start = ((y // 2) * GROUP * 2 + y % 2) * planes + x
            target[first + x, pl.ds(y * GROUP, GROUP), :] = source[
                pl.ds(start, GROUP, stride=2 * planes), :
            ]
        return carry

    lax.fori_loop(0, planes, step, 0, unroll=8)


def inner_kernel(scal, own, v_own, kz, s_edge, y1_edge, y2_edge, y3_inner, own_f, u, s, y1, y2, y3):
    scale = scal[0]
    u[pl.ds(HALO * NY, OWN * NY)] = (v_own[...] + scal[1]) * scale
    own_f[...] = own[...].astype(jnp.float32)
    bring(own_f, OWN, s, 0)
    level(kz, u, scale, None, s, 24, None, 0, y1, 30, 30, 82, 26, start=True)
    level(kz, u, scale, None, y1, 30, s, 24, y2, 36, 36, 76, 20)
    level(kz, u, scale, None, y2, 36, y1, 30, y3, 42, 42, 70, 28)
    for ref, edge in ((s, s_edge), (y1, y1_edge), (y2, y2_edge)):
        edge[0] = ref[pl.ds(0, EDGE)]
        edge[1] = ref[pl.ds(ref.shape[0] - EDGE, EDGE)]
    y3_inner[...] = y3[...].astype(jnp.bfloat16)


def outer_kernel(
    scal, base, left, right, v_own, s_edge, y1_edge, y2_edge, y3_inner, kz,
    out, side_f, u, s, y1, y2, y3,
):
    scale = scal[0]
    v_rows = HALO * NY
    u[pl.ds(v_rows, OWN * NY)] = (v_own[...] + scal[1]) * scale
    y3[pl.ds(18, 28)] = y3_inner[...].astype(jnp.float32)
    for side, halo in ((0, left), (1, right)):
        field_rows = ROWS * HALO
        side_f[...] = halo[...].astype(jnp.float32)
        v = side_f[pl.ds(field_rows, v_rows)] + side_f[pl.ds(field_rows + v_rows, v_rows)]
        u[pl.ds(side * (HALO + OWN) * NY, v_rows)] = (v + scal[1]) * scale
        halo_at, edge_at = ((0, HALO), (EDGE, 0))[side]
        bring(side_f, HALO, s, halo_at)
        s[pl.ds(edge_at, EDGE)] = s_edge[side]
        y1_at, y2_at = ((18, 18), (0, 0))[side]
        y1[pl.ds(y1_at, EDGE)] = y1_edge[side]
        y2[pl.ds(y2_at, EDGE)] = y2_edge[side]
        if side == 0:
            level(kz, u, scale, base, s, 0, None, 0, y1, 12, 12, 30, 18, start=True)
            level(kz, u, scale, base, y1, 12, s, 0, y2, 18, 18, 36, 18)
            level(kz, u, scale, base, y2, 18, y1, 12, y3, 24, 24, 42, 18)
        else:
            level(kz, u, scale, base, s, 76, None, 0, y1, 70, 82, 106, 24, start=True)
            level(kz, u, scale, base, y1, 70, s, 76, y2, 64, 76, 100, 24)
            level(kz, u, scale, base, y2, 64, y1, 70, y3, 24, 70, 94, 24)
    for dest in range(OWN // SLAB):
        out[dest] = y3[pl.ds(dest * SLAB, SENT)].astype(jnp.bfloat16)


def z_both():
    high, low = z_matrix(2)
    return jnp.asarray(np.block([[high, low], [high, np.zeros_like(high)]]))


def inner_planes(scal, own, v_own):
    smem = pl.BlockSpec(memory_space=pltpu.SMEM)
    vmem = pl.BlockSpec(memory_space=pltpu.VMEM)
    f32 = jnp.float32
    edge = jax.ShapeDtypeStruct((2, EDGE, ROWS, NZ), f32)
    return pl.pallas_call(
        inner_kernel,
        out_shape=(edge, edge, edge, jax.ShapeDtypeStruct((28, ROWS, NZ), jnp.bfloat16)),
        in_specs=[smem] + [vmem] * 3,
        out_specs=[vmem] * 4,
        scratch_shapes=[
            pltpu.VMEM((ROWS * OWN, NZ), f32),
            pltpu.VMEM((SPAN * NY, NZ), f32),
            pltpu.VMEM((64, ROWS, NZ), f32),
            pltpu.VMEM((52, ROWS, NZ), f32),
            pltpu.VMEM((40, ROWS, NZ), f32),
            pltpu.VMEM((28, ROWS, NZ), f32),
        ],
        compiler_params=pltpu.CompilerParams(vmem_limit_bytes=VMEM_LIMIT),
        cost_estimate=pl.CostEstimate(
            flops=2_000_000_000, bytes_accessed=8_000_000, transcendentals=0
        ),
        name="filter_inner",
    )(scal, own, v_own, z_both())


def outer_planes(scal, base, left, right, v_own, inner):
    smem = pl.BlockSpec(memory_space=pltpu.SMEM)
    vmem = pl.BlockSpec(memory_space=pltpu.VMEM)
    f32 = jnp.float32
    return pl.pallas_call(
        outer_kernel,
        out_shape=jax.ShapeDtypeStruct((OWN // SLAB, SENT, ROWS, NZ), jnp.bfloat16),
        in_specs=[smem, smem] + [vmem] * 8,
        out_specs=vmem,
        scratch_shapes=[
            pltpu.VMEM(left.shape, f32),
            pltpu.VMEM((SPAN * NY, NZ), f32),
            pltpu.VMEM((36, ROWS, NZ), f32),
            pltpu.VMEM((36, ROWS, NZ), f32),
            pltpu.VMEM((36, ROWS, NZ), f32),
            pltpu.VMEM((70, ROWS, NZ), f32),
        ],
        compiler_params=pltpu.CompilerParams(vmem_limit_bytes=VMEM_LIMIT),
        name="filter_outer",
    )(scal, base, left, right, v_own, *inner, z_both())


def sums_kernel(planes, v, kz, out, fields_out, cells_f, total):
    def unpack(x, carry):
        for g in range(BANDS // GROUP):
            part = planes[g, x].astype(jnp.float32).reshape(NY, GROUP, NZ)
            cells_f[x, :, pl.ds(g * GROUP, GROUP), :] = part
        return carry

    lax.fori_loop(0, SENT, unpack, 0)
    total[...] = jnp.zeros_like(total)

    def step(t, carry):
        x0 = t * PLANES
        block = cells_f[pl.ds(x0, PLANES)].reshape(PLANES * NY * BANDS, NZ)
        block16 = block.astype(jnp.bfloat16)
        z = jnp.dot(block16, kz[...], preferred_element_type=jnp.float32)
        add = total[...]
        for p in range(PLANES):
            x = x0 + p
            at = [slice((p * NY + y) * BANDS, (p * NY + y + 1) * BANDS) for y in range(NY)]
            images = []
            for y in range(NY):
                image = None
                for k in range(1, 7):
                    pair = cells_f[x + k, y]
                    if y + k < NY:
                        pair = pair + block[at[y + k]]
                    pair = SIDE[k - 1] * pair
                    image = pair if image is None else image + pair
                local = jnp.broadcast_to(v[x, pl.ds(y, 1), :], (BANDS, NZ))
                image = image + (0.5 * (local + CENTRE)) * block[at[y]]
                images.append(split_bf16(image + (z[at[y], :NZ] + z[at[y], NZ:])))
            fields = jnp.concatenate([block16[a] for a in at], axis=1)
            fields_out[x] = fields
            highs = jnp.concatenate([i[0] for i in images], axis=1)
            lows = jnp.concatenate([i[1] for i in images], axis=1)
            add = add + lax.dot_general(
                jnp.concatenate([fields, highs, lows], axis=0), fields,
                (((1,), (1,)), ((), ())), preferred_element_type=jnp.float32,
            )
        total[...] = add
        return carry

    lax.fori_loop(0, SLAB // PLANES, step, 0)
    sums = total[...]
    gram = sums[:BANDS]
    half = sums[BANDS : 2 * BANDS] + sums[2 * BANDS :]
    both = jnp.concatenate([gram, half], axis=1)
    row = jnp.concatenate([both[:16], both[16:]], axis=1)
    for copy in range(out.shape[0]):
        out[copy] = row


def matrix_sums(planes, v, copies):
    kz = jnp.asarray(np.concatenate(z_matrix(1), axis=1))
    vmem = pl.BlockSpec(memory_space=pltpu.VMEM)
    f32 = jnp.float32
    return pl.pallas_call(
        sums_kernel,
        out_shape=(
            jax.ShapeDtypeStruct((copies, 16, NZ), f32),
            jax.ShapeDtypeStruct((SLAB, BANDS, NY * NZ), jnp.bfloat16),
        ),
        in_specs=[vmem] * 3,
        out_specs=(vmem, vmem),
        scratch_shapes=[
            pltpu.VMEM((SENT, NY, BANDS, NZ), f32),
            pltpu.VMEM((3 * BANDS, BANDS), f32),
        ],
        compiler_params=pltpu.CompilerParams(vmem_limit_bytes=VMEM_LIMIT),
        name="matrix_sums",
    )(planes, v, kz)


def rotate_kernel(count, parts, fields, out, projected, turned):
    sums = jnp.sum(parts[...], axis=0) * (1.0 / count)
    gram = jnp.concatenate([sums[:, :32], sums[:, 64:96]], axis=0)
    half = jnp.concatenate([sums[:, 32:64], sums[:, 96:]], axis=0)
    ham = half + half.T
    rows = lax.broadcasted_iota(jnp.int32, (BANDS, BANDS), 0)
    columns = lax.broadcasted_iota(jnp.int32, (BANDS, BANDS), 1)
    unit = jnp.where(rows == columns, 1.0, 0.0).astype(jnp.float32)
    work = jnp.concatenate([gram, unit], axis=1)
    index = lax.broadcasted_iota(jnp.int32, (BANDS, 1), 0)
    def column(k):
        return jnp.broadcast_to(work[:, k : k + 1], (BANDS, 2 * BANDS))

    now, after = column(0), column(1)
    for k in range(BANDS):
        inverse_pivot = 1.0 / now[k : k + 1]
        lower = jnp.where(index > k, now, 0.0)
        work = work - lower * (work[k : k + 1] * inverse_pivot)
        if k + 1 < BANDS:
            now = after - lower * (after[k : k + 1] * inverse_pivot)
        if k + 2 < BANDS:
            after = column(k + 2)
    pivots = jnp.sum(jnp.where(rows == columns, work[:, :BANDS], 0.0), axis=1, keepdims=True)
    inverse = work[:, BANDS:] / jnp.sqrt(pivots)
    high = lax.Precision.HIGHEST
    left = jnp.dot(inverse, ham, precision=high, preferred_element_type=jnp.float32)
    projected[...] = lax.dot_general(
        left, inverse, (((1,), (1,)), ((), ())), precision=high,
        preferred_element_type=jnp.float32,
    )
    both = jnp.concatenate(split_bf16(inverse), axis=1)

    def turn(x, carry):
        data = fields[x]
        data = jnp.concatenate([data, data], axis=0)
        result = jnp.dot(both, data, preferred_element_type=jnp.float32)
        for y in range(NY):
            start = pl.multiple_of((x * NY + y) * BANDS, BANDS)
            turned[pl.ds(start, BANDS), :] = result[:, y * NZ : (y + 1) * NZ]
        return carry

    lax.fori_loop(0, SLAB, turn, 0)

    def give(b, carry):
        owner = (lax.rem(b, 4) * 2 + lax.div(b, 4)) * 16
        for pair in range(NY // 2):
            for g in range(BANDS // GROUP):
                for odd in range(2):
                    start = (2 * pair + odd) * BANDS + g * GROUP + b
                    value = turned[pl.ds(start, SLAB, stride=NY * BANDS), :]
                    out[owner + pair * 4 + g, odd] = value.astype(jnp.bfloat16)
        return carry

    lax.fori_loop(0, GROUP, give, 0)


def rotated_planes(parts, fields, count):
    vmem = pl.BlockSpec(memory_space=pltpu.VMEM)

    def kernel(*refs):
        rotate_kernel(count, *refs)

    return pl.pallas_call(
        kernel,
        out_shape=(
            jax.ShapeDtypeStruct((128, 2, SLAB, NZ), jnp.bfloat16),
            jax.ShapeDtypeStruct((BANDS, BANDS), jnp.float32),
        ),
        in_specs=[vmem] * 2,
        out_specs=(vmem, vmem),
        scratch_shapes=[pltpu.VMEM((SLAB * NY * BANDS, NZ), jnp.float32)],
        compiler_params=pltpu.CompilerParams(vmem_limit_bytes=VMEM_LIMIT),
        name="rotate_planes",
    )(parts, fields)


def local(orbitals, potential, cutoff, ceiling):
    x_cells = orbitals.shape[1]
    block_count = x_cells // OWN
    center = 0.5 * (ceiling[0] + cutoff[0])
    half_width = 0.5 * (ceiling[0] - cutoff[0])
    scal = jnp.stack([2.0 / half_width, CENTRE - center])
    block_index = lax.axis_index(BLOCKS)
    base = jnp.stack([block_index * OWN - HALO, jnp.int32(x_cells)])
    place = [z * 4 + y for y in range(4) for z in range(8)]
    up = [(place[i], place[i + 1]) for i in range(block_count - 1)]
    down = [(b, a) for a, b in up]

    x_index = lax.axis_index("x")
    slabs = [
        lax.ppermute(
            potential,
            ("x", "y"),
            [(y * 4 + (x + j) % 4, x * 4 + y) for x in range(4) for y in range(4)],
        )
        for j in range(4)
    ]
    v_slab = slabs[0]
    v_own = lax.dynamic_slice_in_dim(
        jnp.concatenate(slabs[1:] + slabs), (3 - x_index) * SLAB, OWN, axis=0
    )

    chunks = orbitals.reshape(2, block_count, OWN, NZ).swapaxes(0, 1)
    own = lax.all_to_all(chunks, BLOCKS, split_axis=0, concat_axis=0, tiled=True)
    def with_potential(field, v):
        parts = [p.reshape(HALO * NY, NZ) for p in split_bf16(v)]
        return jnp.concatenate([field.reshape(ROWS * HALO, NZ)] + parts, axis=0)

    tail = with_potential(own[:, :, OWN - HALO :], v_own[OWN - HALO :])
    head = with_potential(own[:, :, :HALO], v_own[:HALO])
    left = lax.ppermute(tail, ("h", "l", "y"), up)
    right = lax.ppermute(head, ("h", "l", "y"), down)
    v_rows = v_own.reshape(OWN * NY, NZ)
    inner = inner_planes(scal, own.reshape(ROWS * OWN, NZ), v_rows)
    filtered = outer_planes(scal, base, left, right, v_rows, inner)
    planes = lax.all_to_all(filtered, "x", split_axis=0, concat_axis=0, tiled=True)
    sums, fields = matrix_sums(planes, v_slab, 16)
    sums = lax.all_to_all(sums, ("x", "y"), split_axis=0, concat_axis=0, tiled=True)
    sums = jnp.broadcast_to(jnp.sum(sums, axis=0)[None], (8, 16, NZ))
    sums = lax.all_to_all(sums, ("l", "h"), split_axis=0, concat_axis=0, tiled=True)
    rotated, projected = rotated_planes(sums, fields, x_cells * NY * NZ)
    returned = lax.all_to_all(
        rotated, ("l", "h", "y", "x"), split_axis=0, concat_axis=0, tiled=True
    )
    returned = returned.reshape(4, 2, 4, 4, 2, SLAB, NZ).transpose(4, 2, 1, 0, 3, 5, 6)
    returned = returned.reshape(2, x_cells, NZ)
    return (returned, projected)


def solution(mesh):
    mesh = Mesh(mesh.devices.reshape(2, 4, 2, 4, 4), ("spin",) + DOM)
    return jax.shard_map(
        local,
        mesh=mesh,
        in_specs=(
            P(("spin",) + DOM, None, None),
            P(("spin",) + DOM, None, None),
            P("spin"),
            P("spin"),
        ),
        out_specs=(P(("spin",) + DOM, None, None), P("spin", None)),
        check_vma=False,
    )
```

```python
import jax
import jax.numpy as jnp
import numpy as np
from jax import lax
from jax.experimental import pallas as pl
from jax.experimental.pallas import tpu as pltpu
from jax.sharding import Mesh, PartitionSpec as P

DOM = ("x", "h", "l", "y")
BLOCKS = ("y", "h", "l")

STENCIL = (
    -5369.0 / 1800.0,
    12.0 / 7.0,
    -15.0 / 56.0,
    10.0 / 189.0,
    -1.0 / 112.0,
    2.0 / 1925.0,
    -1.0 / 16632.0,
)
KINETIC = -2.0
SIDE = tuple(KINETIC * c for c in STENCIL[1:])
CENTRE = KINETIC * 3.0 * STENCIL[0]

NY = 8
NZ = 128
GROUP = 8
BANDS = 32
OWN = 64
HALO = 24
SPAN = OWN + 2 * HALO
SLAB = 16
AHEAD = 6
SENT = SLAB + AHEAD
ROWS = NY * GROUP
EDGE = 12
PLANES = 8
VMEM_LIMIT = 18 * 1024 * 1024


def split_bf16(value):
    high = value.astype(jnp.bfloat16)
    low = (value - high.astype(jnp.float32)).astype(jnp.bfloat16)
    return high, low


def z_matrix(sides):
    band = np.zeros((NZ, NZ), np.float64)
    for offset in range(1, 7):
        for cell in range(NZ - offset):
            band[cell + offset, cell] = SIDE[offset - 1]
            if sides == 2:
                band[cell, cell + offset] = SIDE[offset - 1]
    band = band.astype(np.float32)
    high = band.astype(jnp.bfloat16)
    low = (band - high.astype(np.float32)).astype(jnp.bfloat16)
    return high, low


def level(
    kz, u, scale, base, source, source_first, before, before_first,
    target, target_first, first, last, count, start=False,
):
    def step(t, carry):
        i = first + count * t
        at = i - source_first
        block = source[pl.ds(at, count)].reshape(count * ROWS, NZ)
        if start:
            z = jnp.dot(block.astype(jnp.bfloat16), kz[:NZ], preferred_element_type=jnp.float32)
        else:
            z = jnp.dot(
                jnp.concatenate(split_bf16(block), axis=1), kz[...],
                preferred_element_type=jnp.float32,
            )
        for p in range(count):
            factor = scale
            if base is not None:
                plane = base[0] + i + p
                factor = jnp.where((plane >= 0) & (plane < base[1]), scale, 0.0)
            at_y = [slice(p * ROWS + y * GROUP, p * ROWS + (y + 1) * GROUP) for y in range(NY)]
            for y in range(NY):
                here = pl.ds(y * GROUP, GROUP)
                total = None
                for k in range(1, 7):
                    pair = source[at + p + k, here, :] + source[at + p - k, here, :]
                    if y + k < NY:
                        pair = pair + block[at_y[y + k]]
                    if y - k >= 0:
                        pair = pair + block[at_y[y - k]]
                    pair = SIDE[k - 1] * pair
                    total = pair if total is None else total + pair
                total = total + (z[at_y[y], :NZ] + z[at_y[y], NZ:])
                local = jnp.broadcast_to(u[pl.ds((i + p) * NY + y, 1), :], (GROUP, NZ))
                value = factor * total + local * block[at_y[y]]
                if start:
                    value = 0.5 * value
                else:
                    value = value - before[i + p - before_first, here, :]
                target[i + p - target_first, here, :] = value
        return carry

    lax.fori_loop(0, (last - first) // count, step, 0)


def bring(source, planes, target, first):
    def step(x, carry):
        for y in range(NY):
            start = ((y // 2) * GROUP * 2 + y % 2) * planes + x
            target[first + x, pl.ds(y * GROUP, GROUP), :] = source[
                pl.ds(start, GROUP, stride=2 * planes), :
            ]
        return carry

    lax.fori_loop(0, planes, step, 0, unroll=8)


def inner_kernel(scal, own, v_own, kz, s_edge, y1_edge, y2_edge, y3_inner, own_f, u, s, y1, y2, y3):
    scale = scal[0]
    u[pl.ds(HALO * NY, OWN * NY)] = (v_own[...] + scal[1]) * scale
    own_f[...] = own[...].astype(jnp.float32)
    bring(own_f, OWN, s, 0)
    level(kz, u, scale, None, s, 24, None, 0, y1, 30, 30, 82, 26, start=True)
    level(kz, u, scale, None, y1, 30, s, 24, y2, 36, 36, 76, 20)
    level(kz, u, scale, None, y2, 36, y1, 30, y3, 42, 42, 70, 28)
    for ref, edge in ((s, s_edge), (y1, y1_edge), (y2, y2_edge)):
        edge[0] = ref[pl.ds(0, EDGE)]
        edge[1] = ref[pl.ds(ref.shape[0] - EDGE, EDGE)]
    y3_inner[...] = y3[...].astype(jnp.bfloat16)


def outer_kernel(
    scal, base, left, right, v_own, s_edge, y1_edge, y2_edge, y3_inner, kz,
    out, side_f, u, s, y1, y2, y3,
):
    scale = scal[0]
    v_rows = HALO * NY
    u[pl.ds(v_rows, OWN * NY)] = (v_own[...] + scal[1]) * scale
    y3[pl.ds(18, 28)] = y3_inner[...].astype(jnp.float32)
    for side, halo in ((0, left), (1, right)):
        field_rows = ROWS * HALO
        side_f[...] = halo[...].astype(jnp.float32)
        v = side_f[pl.ds(field_rows, v_rows)]
        u[pl.ds(side * (HALO + OWN) * NY, v_rows)] = (v + scal[1]) * scale
        halo_at, edge_at = ((0, HALO), (EDGE, 0))[side]
        bring(side_f, HALO, s, halo_at)
        s[pl.ds(edge_at, EDGE)] = s_edge[side]
        y1_at, y2_at = ((18, 18), (0, 0))[side]
        y1[pl.ds(y1_at, EDGE)] = y1_edge[side]
        y2[pl.ds(y2_at, EDGE)] = y2_edge[side]
        if side == 0:
            level(kz, u, scale, base, s, 0, None, 0, y1, 12, 12, 30, 18, start=True)
            level(kz, u, scale, base, y1, 12, s, 0, y2, 18, 18, 36, 18)
            level(kz, u, scale, base, y2, 18, y1, 12, y3, 24, 24, 42, 18)
        else:
            level(kz, u, scale, base, s, 76, None, 0, y1, 70, 82, 106, 24, start=True)
            level(kz, u, scale, base, y1, 70, s, 76, y2, 64, 76, 100, 24)
            level(kz, u, scale, base, y2, 64, y1, 70, y3, 24, 70, 94, 24)
    for dest in range(OWN // SLAB):
        out[dest] = y3[pl.ds(dest * SLAB, SENT)].astype(jnp.bfloat16)


def z_both():
    high, low = z_matrix(2)
    return jnp.asarray(np.block([[high, low], [high, np.zeros_like(high)]]))


def inner_planes(scal, own, v_own):
    smem = pl.BlockSpec(memory_space=pltpu.SMEM)
    vmem = pl.BlockSpec(memory_space=pltpu.VMEM)
    f32 = jnp.float32
    edge = jax.ShapeDtypeStruct((2, EDGE, ROWS, NZ), f32)
    return pl.pallas_call(
        inner_kernel,
        out_shape=(edge, edge, edge, jax.ShapeDtypeStruct((28, ROWS, NZ), jnp.bfloat16)),
        in_specs=[smem] + [vmem] * 3,
        out_specs=[vmem] * 4,
        scratch_shapes=[
            pltpu.VMEM((ROWS * OWN, NZ), f32),
            pltpu.VMEM((SPAN * NY, NZ), f32),
            pltpu.VMEM((64, ROWS, NZ), f32),
            pltpu.VMEM((52, ROWS, NZ), f32),
            pltpu.VMEM((40, ROWS, NZ), f32),
            pltpu.VMEM((28, ROWS, NZ), f32),
        ],
        compiler_params=pltpu.CompilerParams(vmem_limit_bytes=VMEM_LIMIT),
        cost_estimate=pl.CostEstimate(
            flops=2_000_000_000, bytes_accessed=8_000_000, transcendentals=0
        ),
        name="filter_inner",
    )(scal, own, v_own, z_both())


def outer_planes(scal, base, left, right, v_own, inner):
    smem = pl.BlockSpec(memory_space=pltpu.SMEM)
    vmem = pl.BlockSpec(memory_space=pltpu.VMEM)
    f32 = jnp.float32
    return pl.pallas_call(
        outer_kernel,
        out_shape=jax.ShapeDtypeStruct((OWN // SLAB, SENT, ROWS, NZ), jnp.bfloat16),
        in_specs=[smem, smem] + [vmem] * 8,
        out_specs=vmem,
        scratch_shapes=[
            pltpu.VMEM(left.shape, f32),
            pltpu.VMEM((SPAN * NY, NZ), f32),
            pltpu.VMEM((36, ROWS, NZ), f32),
            pltpu.VMEM((36, ROWS, NZ), f32),
            pltpu.VMEM((36, ROWS, NZ), f32),
            pltpu.VMEM((70, ROWS, NZ), f32),
        ],
        compiler_params=pltpu.CompilerParams(vmem_limit_bytes=VMEM_LIMIT),
        name="filter_outer",
    )(scal, base, left, right, v_own, *inner, z_both())


def sums_kernel(planes, v, kz, out, fields_out, cells_f, total):
    def unpack(x, carry):
        for g in range(BANDS // GROUP):
            part = planes[g, x].astype(jnp.float32).reshape(NY, GROUP, NZ)
            cells_f[x, :, pl.ds(g * GROUP, GROUP), :] = part
        return carry

    lax.fori_loop(0, SENT, unpack, 0)
    total[...] = jnp.zeros_like(total)

    def step(t, carry):
        x0 = t * PLANES
        block = cells_f[pl.ds(x0, PLANES)].reshape(PLANES * NY * BANDS, NZ)
        block16 = block.astype(jnp.bfloat16)
        z = jnp.dot(block16, kz[...], preferred_element_type=jnp.float32)
        add = total[...]
        for p in range(PLANES):
            x = x0 + p
            at = [slice((p * NY + y) * BANDS, (p * NY + y + 1) * BANDS) for y in range(NY)]
            images = []
            for y in range(NY):
                image = None
                for k in range(1, 7):
                    pair = cells_f[x + k, y]
                    if y + k < NY:
                        pair = pair + block[at[y + k]]
                    pair = SIDE[k - 1] * pair
                    image = pair if image is None else image + pair
                local = jnp.broadcast_to(v[x, pl.ds(y, 1), :], (BANDS, NZ))
                image = image + (0.5 * (local + CENTRE)) * block[at[y]]
                images.append(split_bf16(image + (z[at[y], :NZ] + z[at[y], NZ:])))
            fields = jnp.concatenate([block16[a] for a in at], axis=1)
            fields_out[x] = fields
            highs = jnp.concatenate([i[0] for i in images], axis=1)
            lows = jnp.concatenate([i[1] for i in images], axis=1)
            add = add + lax.dot_general(
                jnp.concatenate([fields, highs, lows], axis=0), fields,
                (((1,), (1,)), ((), ())), preferred_element_type=jnp.float32,
            )
        total[...] = add
        return carry

    lax.fori_loop(0, SLAB // PLANES, step, 0)
    sums = total[...]
    gram = sums[:BANDS]
    half = sums[BANDS : 2 * BANDS] + sums[2 * BANDS :]
    both = jnp.concatenate([gram, half], axis=1)
    row = jnp.concatenate([both[:16], both[16:]], axis=1)
    for copy in range(out.shape[0]):
        out[copy] = row


def matrix_sums(planes, v, copies):
    kz = jnp.asarray(np.concatenate(z_matrix(1), axis=1))
    vmem = pl.BlockSpec(memory_space=pltpu.VMEM)
    f32 = jnp.float32
    return pl.pallas_call(
        sums_kernel,
        out_shape=(
            jax.ShapeDtypeStruct((copies, 16, NZ), f32),
            jax.ShapeDtypeStruct((SLAB, BANDS, NY * NZ), jnp.bfloat16),
        ),
        in_specs=[vmem] * 3,
        out_specs=(vmem, vmem),
        scratch_shapes=[
            pltpu.VMEM((SENT, NY, BANDS, NZ), f32),
            pltpu.VMEM((3 * BANDS, BANDS), f32),
        ],
        compiler_params=pltpu.CompilerParams(vmem_limit_bytes=VMEM_LIMIT),
        name="matrix_sums",
    )(planes, v, kz)


def rotate_kernel(count, parts, fields, out, projected, turned):
    sums = jnp.sum(parts[...], axis=0) * (1.0 / count)
    gram = jnp.concatenate([sums[:, :32], sums[:, 64:96]], axis=0)
    half = jnp.concatenate([sums[:, 32:64], sums[:, 96:]], axis=0)
    ham = half + half.T
    rows = lax.broadcasted_iota(jnp.int32, (BANDS, BANDS), 0)
    columns = lax.broadcasted_iota(jnp.int32, (BANDS, BANDS), 1)
    unit = jnp.where(rows == columns, 1.0, 0.0).astype(jnp.float32)
    work = jnp.concatenate([gram, unit], axis=1)
    index = lax.broadcasted_iota(jnp.int32, (BANDS, 1), 0)
    def column(k):
        return jnp.broadcast_to(work[:, k : k + 1], (BANDS, 2 * BANDS))

    now, after = column(0), column(1)
    for k in range(BANDS):
        inverse_pivot = 1.0 / now[k : k + 1]
        lower = jnp.where(index > k, now, 0.0)
        work = work - lower * (work[k : k + 1] * inverse_pivot)
        if k + 1 < BANDS:
            now = after - lower * (after[k : k + 1] * inverse_pivot)
        if k + 2 < BANDS:
            after = column(k + 2)
    pivots = jnp.sum(jnp.where(rows == columns, work[:, :BANDS], 0.0), axis=1, keepdims=True)
    inverse = work[:, BANDS:] / jnp.sqrt(pivots)
    high = lax.Precision.HIGHEST
    left = jnp.dot(inverse, ham, precision=high, preferred_element_type=jnp.float32)
    projected[...] = lax.dot_general(
        left, inverse, (((1,), (1,)), ((), ())), precision=high,
        preferred_element_type=jnp.float32,
    )
    both = jnp.concatenate(split_bf16(inverse), axis=1)

    def turn(x, carry):
        data = fields[x]
        data = jnp.concatenate([data, data], axis=0)
        result = jnp.dot(both, data, preferred_element_type=jnp.float32)
        for y in range(NY):
            start = pl.multiple_of((x * NY + y) * BANDS, BANDS)
            turned[pl.ds(start, BANDS), :] = result[:, y * NZ : (y + 1) * NZ]
        return carry

    lax.fori_loop(0, SLAB, turn, 0, unroll=4)

    def give(b, carry):
        owner = (lax.rem(b, 4) * 2 + lax.div(b, 4)) * 16
        for pair in range(NY // 2):
            for g in range(BANDS // GROUP):
                for odd in range(2):
                    start = (2 * pair + odd) * BANDS + g * GROUP + b
                    value = turned[pl.ds(start, SLAB, stride=NY * BANDS), :]
                    out[owner + pair * 4 + g, odd] = value.astype(jnp.bfloat16)
        return carry

    lax.fori_loop(0, GROUP, give, 0, unroll=2)


def rotated_planes(parts, fields, count):
    vmem = pl.BlockSpec(memory_space=pltpu.VMEM)

    def kernel(*refs):
        rotate_kernel(count, *refs)

    return pl.pallas_call(
        kernel,
        out_shape=(
            jax.ShapeDtypeStruct((128, 2, SLAB, NZ), jnp.bfloat16),
            jax.ShapeDtypeStruct((BANDS, BANDS), jnp.float32),
        ),
        in_specs=[vmem] * 2,
        out_specs=(vmem, vmem),
        scratch_shapes=[pltpu.VMEM((SLAB * NY * BANDS, NZ), jnp.float32)],
        compiler_params=pltpu.CompilerParams(vmem_limit_bytes=VMEM_LIMIT),
        name="rotate_planes",
    )(parts, fields)


def local(orbitals, potential, cutoff, ceiling):
    x_cells = orbitals.shape[1]
    block_count = x_cells // OWN
    center = 0.5 * (ceiling[0] + cutoff[0])
    half_width = 0.5 * (ceiling[0] - cutoff[0])
    scal = jnp.stack([2.0 / half_width, CENTRE - center])
    block_index = lax.axis_index(BLOCKS)
    base = jnp.stack([block_index * OWN - HALO, jnp.int32(x_cells)])
    place = [z * 4 + y for y in range(4) for z in range(8)]
    up = [(place[i], place[i + 1]) for i in range(block_count - 1)]
    down = [(b, a) for a, b in up]

    x_index = lax.axis_index("x")
    slabs = [
        lax.ppermute(
            potential,
            ("x", "y"),
            [(y * 4 + (x + j) % 4, x * 4 + y) for x in range(4) for y in range(4)],
        )
        for j in range(4)
    ]
    v_slab = slabs[0]
    v_own = lax.dynamic_slice_in_dim(
        jnp.concatenate(slabs[1:] + slabs), (3 - x_index) * SLAB, OWN, axis=0
    )

    chunks = orbitals.reshape(2, block_count, OWN, NZ).swapaxes(0, 1)
    own = lax.all_to_all(chunks, BLOCKS, split_axis=0, concat_axis=0, tiled=True)
    def with_potential(field, v):
        v = v.astype(jnp.bfloat16).reshape(HALO * NY, NZ)
        return jnp.concatenate([field.reshape(ROWS * HALO, NZ), v], axis=0)

    tail = with_potential(own[:, :, OWN - HALO :], v_own[OWN - HALO :])
    head = with_potential(own[:, :, :HALO], v_own[:HALO])
    left = lax.ppermute(tail, ("h", "l", "y"), up)
    right = lax.ppermute(head, ("h", "l", "y"), down)
    v_rows = v_own.reshape(OWN * NY, NZ)
    inner = inner_planes(scal, own.reshape(ROWS * OWN, NZ), v_rows)
    filtered = outer_planes(scal, base, left, right, v_rows, inner)
    planes = lax.all_to_all(filtered, "x", split_axis=0, concat_axis=0, tiled=True)
    sums, fields = matrix_sums(planes, v_slab, 16)
    sums = lax.all_to_all(sums, ("x", "y"), split_axis=0, concat_axis=0, tiled=True)
    sums = jnp.broadcast_to(jnp.sum(sums, axis=0)[None], (8, 16, NZ))
    sums = lax.all_to_all(sums, ("l", "h"), split_axis=0, concat_axis=0, tiled=True)
    rotated, projected = rotated_planes(sums, fields, x_cells * NY * NZ)
    returned = lax.all_to_all(
        rotated, ("l", "h", "y", "x"), split_axis=0, concat_axis=0, tiled=True
    )
    returned = returned.reshape(4, 2, 4, 4, 2, SLAB, NZ).transpose(4, 2, 1, 0, 3, 5, 6)
    returned = returned.reshape(2, x_cells, NZ)
    return (returned, projected)


def solution(mesh):
    mesh = Mesh(mesh.devices.reshape(2, 4, 2, 4, 4), ("spin",) + DOM)
    return jax.shard_map(
        local,
        mesh=mesh,
        in_specs=(
            P(("spin",) + DOM, None, None),
            P(("spin",) + DOM, None, None),
            P("spin"),
            P("spin"),
        ),
        out_specs=(P(("spin",) + DOM, None, None), P("spin", None)),
        check_vma=False,
    )
```
